32 devices in a mesh: row: 4 (over z), col: 8 (over y, x, core).
Axes of the slice: x: 2, y: 2, z: 4, core: 2. Of those that a mesh axis runs over, the one named last changes fastest.
Arguments:
- right_side: float32 [4096, 4, 128], P(('row', 'col')), may hold values from -60 to 60
- cluster_of: int32 [4096], P(('row', 'col')), may hold values from 0 to 4095, as said below
- near_rows: int32 [12288], P(('row', 'col')), may hold values from 0 to 127
- near_columns: int32 [12288], P(('row', 'col')), may hold values from 0 to 191, as said below
- near_blocks: bfloat16 [12288, 128, 128], P(('row', 'col')), may hold values from -1 to 1
- far_rows: int32 [32768], P(('row', 'col')), may hold values from 0 to 1023, as said below
- far_columns: int32 [32768], P(('row', 'col')), may hold values from 0 to 511
- far_rank: int32 [32768], P(('row', 'col')), may hold values from 4 to 16
- far_left: bfloat16 [32768, 16, 128], P(('row', 'col')), may hold values from -1.5 to 1.5
- far_right: bfloat16 [32768, 16, 128], P(('row', 'col')), may hold values from -0.5 to 0.5
Outputs:
- second_basis: float32 [4096, 4, 128], P(('row', 'col'))
- next_vector: float32 [4096, 4, 128], P(('row', 'col'))
- hessenberg: float32 [5, 4], replicated
The draws below stay inside these ranges and needn't reach their ends.
Inputs may be any that keep to these rules, and one draw needn't show every extreme that they name: `cluster_of`: A permutation of the cluster positions; position g belongs to the device of index g // 128 along row+col. Each device's blocks go to at most 8 blocks a destination device, and exactly 8 to some. `near_columns`: position 32 is the device's own first block; entries never point before the first or after the last block of cluster order. `far_rows`: in each device's list, the k-th group of 128 entries has rows in blocks k * 128 to (k + 1) * 128 - 1 of the row cluster.
All inputs are finite; a program needn't handle non-finite values.
Results may differ from the reference program's by a relative error of at most 0.0018.
The reference program's roundings to bfloat16 on the way (of `clustered` and `coefficients`) count: a program that leaves them out, or rounds other values in their place, can miss the bound.
Values may be sent and summed in bfloat16 or wider, within the bound.
A program may use at most 128 MiB of HBM per device.

```python
import math
import jax
import jax.numpy as jnp
from jax import lax

BLOCK_SIZE = 128
MAX_RANK = 16
SIDES = 4
BLOCKS_DEV = 128
NEAR_DEV = 384
FAR_DEV = 1024
BLOCKS = 4096
PANELS = 524288
CAPACITY = 8
HALO_BLOCKS = 32
ROW_CLUSTER = 1024
COL_CLUSTER = 512
FAR_GROUP = 128
N_COL = 8
DEVICES = 32


def draw_right_side(key, part):
    key_base, key_block, key_side = jax.random.split(key, 3)
    index = jnp.arange(BLOCKS, dtype=jnp.float32)
    rising = 0.5 + index / BLOCKS
    block_scale = jnp.exp(jax.random.uniform(key_block, (BLOCKS,), jnp.float32, math.log(0.6), math.log(2.4)))
    side_scale = jnp.exp(jax.random.uniform(key_side, (SIDES,), jnp.float32, math.log(0.3), math.log(3.0)))
    values = jnp.clip(jax.random.normal(key_base, (BLOCKS, SIDES, BLOCK_SIZE), jnp.float32), -3.0, 3.0)
    return values * (rising * block_scale)[:, None, None] * side_scale[None, :, None]


def draw_cluster_of(key, part):
    key_shift, key_source, key_target = jax.random.split(jax.random.fold_in(key, 7), 3)
    shifts = jax.random.permutation(key_shift, DEVICES).astype(jnp.int32)

    def one_order(single_key):
        return jax.random.permutation(single_key, BLOCKS_DEV).astype(jnp.int32)
    source_order = jax.vmap(one_order)(jax.random.split(key_source, DEVICES))
    target_order = jax.vmap(one_order)(jax.random.split(key_target, DEVICES))
    heavy = DEVICES // 4 * CAPACITY
    group = jnp.where(source_order < heavy, source_order // CAPACITY, DEVICES // 4 + (source_order - heavy) // (CAPACITY // 2))
    source = jnp.arange(DEVICES, dtype=jnp.int32)[:, None]
    target = (source + shifts[group]) % DEVICES
    position = target * BLOCKS_DEV + target_order[target, source_order]
    return position.reshape(-1).astype(jnp.int32)


def near_pairs(key):
    key_rows, key_offsets = jax.random.split(jax.random.fold_in(key, 11), 2)
    rows = jax.random.randint(key_rows, (DEVICES, NEAR_DEV), 0, BLOCKS_DEV).astype(jnp.int32)
    offsets = jax.random.randint(key_offsets, (DEVICES, NEAR_DEV), -HALO_BLOCKS, HALO_BLOCKS + 1).astype(jnp.int32)
    entry = jnp.arange(NEAR_DEV, dtype=jnp.int32)
    self_entry = (entry % 3 == 2) & ((entry - 2) // 3 < BLOCKS_DEV)
    rows = jnp.where(self_entry[None, :], ((entry - 2) // 3)[None, :], rows).astype(jnp.int32)
    offsets = jnp.where(self_entry[None, :], 0, offsets).astype(jnp.int32)
    rows = rows.at[:, 0].set(BLOCKS_DEV - 1).at[:, 1].set(0)
    offsets = offsets.at[:, 0].set(HALO_BLOCKS).at[:, 1].set(-HALO_BLOCKS)
    relative = rows + offsets
    device = jnp.arange(DEVICES, dtype=jnp.int32)[:, None]
    relative = jnp.where((device == 0) & (relative < 0), -relative - 1, relative)
    relative = jnp.where((device == DEVICES - 1) & (relative >= BLOCKS_DEV), 2 * BLOCKS_DEV - 1 - relative, relative)
    return (rows.reshape(-1), (relative + HALO_BLOCKS).reshape(-1).astype(jnp.int32))


def draw_near_rows(key, part):
    return near_pairs(key)[0]


def draw_near_columns(key, part):
    return near_pairs(key)[1]


def draw_near_blocks(key, part):
    key_noise, key_level, key_entry = jax.random.split(jax.random.fold_in(key, 17), 3)
    sigma = 1.0 / math.sqrt(BLOCK_SIZE)
    shape = (DEVICES * NEAR_DEV, BLOCK_SIZE, BLOCK_SIZE)
    noise = jax.random.normal(key_noise, shape, jnp.float32) * sigma
    noise = jnp.clip(noise, -0.35, 0.35)
    level = jnp.exp(jax.random.uniform(key_level, (DEVICES,), jnp.float32, math.log(0.15), math.log(0.5)))
    factor = jax.random.uniform(key_entry, (DEVICES, NEAR_DEV), jnp.float32, 0.7, 1.3)
    diagonal = (level[:, None] * factor).reshape(-1)
    identity = jnp.eye(BLOCK_SIZE, dtype=jnp.float32)
    return (noise + diagonal[:, None, None] * identity[None, :, :]).astype(jnp.bfloat16)


def draw_far_rows(key, part):
    offsets = jax.random.randint(jax.random.fold_in(key, 13), (DEVICES, FAR_DEV), 0, BLOCKS_DEV).astype(jnp.int32)
    offsets = offsets.at[:, 0].set(0).at[:, FAR_DEV - 1].set(BLOCKS_DEV - 1)
    bucket = jnp.arange(FAR_DEV, dtype=jnp.int32) // FAR_GROUP
    return (bucket[None, :] * BLOCKS_DEV + offsets).reshape(-1).astype(jnp.int32)


def set_ends(result, own_key, low, top_value):
    longest = result.shape.index(max(result.shape))
    spots = []
    for shift in (0, 1):
        where = [jax.random.randint(jax.random.fold_in(own_key, axis), (), 0, length) for axis, length in enumerate(result.shape)]
        where[longest] = (where[longest] + shift) % result.shape[longest]
        spots.append(tuple(where))
    return result.at[spots[0]].set(low).at[spots[1]].set(top_value)


def shard_levels(key, dims, shards, smallest, largest):
    level = 1.0
    for dim, shards_of in shards:
        draws = jax.random.uniform(jax.random.fold_in(jax.random.fold_in(key, 6), dim), (shards_of,), jnp.float32, smallest / len(shards), largest / len(shards))
        level = level * jnp.repeat(jnp.exp(draws), dims[dim] // shards_of).reshape((-1,) + (1,) * (len(dims) - 1 - dim))
    return level


def normal_values(key, shape, spread, reach, shards=(), kind=jnp.bfloat16):
    result = jax.random.normal(key, shape, jnp.float32) * spread
    if len(shards) > 0:
        result = shard_levels(key, shape, shards, -0.22, 0.18) * result
    return jnp.clip(result, min=-reach, max=reach).astype(kind)


def setup_inputs(seed: int = 0) -> dict:
    arg_keys = jax.random.split(jax.random.key(seed), 11)
    right_side = draw_right_side(jax.random.fold_in(arg_keys[10], 71), 0)
    cluster_of = draw_cluster_of(jax.random.fold_in(arg_keys[10], 71), 0)
    near_rows = draw_near_rows(jax.random.fold_in(arg_keys[10], 71), 0)
    near_columns = draw_near_columns(jax.random.fold_in(arg_keys[10], 71), 0)
    near_blocks = draw_near_blocks(jax.random.fold_in(arg_keys[10], 71), 0)
    far_rows = draw_far_rows(jax.random.fold_in(arg_keys[10], 71), 0)
    far_columns = set_ends(jax.random.randint(arg_keys[6], (DEVICES * FAR_DEV,), 0, COL_CLUSTER), jax.random.fold_in(arg_keys[6], 1), 0, COL_CLUSTER - 1).astype(jnp.int32)
    far_rank = set_ends(jax.random.randint(arg_keys[7], (DEVICES * FAR_DEV,), 4, MAX_RANK + 1), jax.random.fold_in(arg_keys[7], 1), 4, MAX_RANK).astype(jnp.int32)
    far_left = normal_values(arg_keys[8], (DEVICES * FAR_DEV, MAX_RANK, BLOCK_SIZE), MAX_RANK ** -0.5, 1.5, ((0, 32),))
    far_right = normal_values(arg_keys[9], (DEVICES * FAR_DEV, MAX_RANK, BLOCK_SIZE), BLOCK_SIZE ** -0.5, 0.5, ((0, 32),))
    return {"right_side": right_side, "cluster_of": cluster_of, "near_rows": near_rows, "near_columns": near_columns, "near_blocks": near_blocks, "far_rows": far_rows, "far_columns": far_columns, "far_rank": far_rank, "far_left": far_left, "far_right": far_right}


epsilon = 1e-06

def apply_operator(vector, cluster_of, near_rows, near_columns, near_blocks, far_rows, far_columns, far_rank, far_left, far_right):
    rounded = lax.optimization_barrier(vector.astype(jnp.bfloat16))
    clustered = jnp.zeros_like(rounded).at[cluster_of].set(rounded)
    padded = jnp.pad(clustered, ((HALO_BLOCKS, HALO_BLOCKS), (0, 0), (0, 0)))
    start_image = 0.5 * clustered.astype(jnp.float32)
    rank_index = jnp.arange(MAX_RANK, dtype=jnp.int32)

    def device_terms(image_sum, scanned):
        device, row_near, column_near, matrix_near, row_far, column_far, ranks_far, left_factor, right_factor = scanned
        offset = device * BLOCKS_DEV
        picked = padded[offset + column_near].astype(jnp.float32)
        near_out = jnp.einsum('ekp,eqp->eqk', matrix_near.astype(jnp.float32), picked, precision=lax.Precision.HIGHEST)
        image_sum = image_sum.at[offset + row_near].add(near_out)
        row_index = device // N_COL
        column_index = device % N_COL
        global_columns = (column_far // BLOCKS_DEV * N_COL + column_index) * BLOCKS_DEV + column_far % BLOCKS_DEV
        far_picked = clustered[global_columns].astype(jnp.float32)
        coefficients = jnp.einsum('etp,eqp->etq', right_factor.astype(jnp.float32), far_picked, precision=lax.Precision.HIGHEST)
        rank_mask = (rank_index[None, :] < ranks_far[:, None]).astype(jnp.float32)
        coefficients = lax.optimization_barrier((coefficients * rank_mask[:, :, None]).astype(jnp.bfloat16))
        far_out = jnp.einsum('etq,etk->eqk', coefficients.astype(jnp.float32), left_factor.astype(jnp.float32), precision=lax.Precision.HIGHEST)
        image_sum = image_sum.at[row_index * ROW_CLUSTER + row_far].add(far_out)
        return (image_sum, None)
    scanned = (jnp.arange(DEVICES, dtype=jnp.int32), near_rows.reshape(DEVICES, NEAR_DEV), near_columns.reshape(DEVICES, NEAR_DEV), near_blocks.reshape(DEVICES, NEAR_DEV, BLOCK_SIZE, BLOCK_SIZE), far_rows.reshape(DEVICES, FAR_DEV), far_columns.reshape(DEVICES, FAR_DEV), far_rank.reshape(DEVICES, FAR_DEV), far_left.reshape(DEVICES, FAR_DEV, MAX_RANK, BLOCK_SIZE), far_right.reshape(DEVICES, FAR_DEV, MAX_RANK, BLOCK_SIZE))
    image_sum, unused = lax.scan(device_terms, start_image, scanned)
    return image_sum[cluster_of]

def inner_mean(left_vector, right_vector):
    return lax.optimization_barrier(jnp.sum(left_vector * right_vector, axis=(0, 2))) / PANELS

def reference(right_side, cluster_of, near_rows, near_columns, near_blocks, far_rows, far_columns, far_rank, far_left, far_right):

    def operate(vector):
        return apply_operator(vector, cluster_of, near_rows, near_columns, near_blocks, far_rows, far_columns, far_rank, far_left, far_right)
    side_norm = jnp.sqrt(inner_mean(right_side, right_side) + epsilon)
    first = right_side / side_norm[None, :, None]
    image_one = operate(first)
    project_one = inner_mean(first, image_one)
    remainder = image_one - project_one[None, :, None] * first
    norm_two = jnp.sqrt(inner_mean(remainder, remainder) + epsilon)
    second_basis = remainder / norm_two[None, :, None]
    image_two = operate(second_basis)
    project_two = inner_mean(first, image_two)
    project_three = inner_mean(second_basis, image_two)
    next_vector = image_two - project_two[None, :, None] * first - project_three[None, :, None] * second_basis
    hessenberg = jnp.stack([side_norm, project_one, norm_two, project_two, project_three])
    return (second_basis, next_vector, hessenberg)
```

```python
import functools

import jax
import jax.numpy as jnp
from jax import lax
from jax.experimental import pallas as pl
from jax.experimental.pallas import tpu as pltpu
from jax.sharding import PartitionSpec as P

epsilon = 1e-06
MESH = pl.DeviceIdType.MESH
HIGH = lax.Precision.HIGHEST
VMEM = pl.BlockSpec(memory_space=pltpu.VMEM)
LANES = 128
LIMIT = 56 * 2**20


def coordinates(index, column_count):
    return (lax.div(index, column_count), lax.rem(index, column_count))


def enter(me, rows, columns):
    count = rows * columns
    barrier = pltpu.get_barrier_semaphore()

    @pl.loop(1, count)
    def _(k):
        pl.semaphore_signal(
            barrier,
            inc=1,
            device_id=coordinates(lax.rem(me + k, count), columns),
            device_id_type=MESH,
        )

    pl.semaphore_wait(barrier, count - 1)


def exchange_kernel(rows, columns, send_ref, recv_ref, send_sem, recv_sem):
    count = rows * columns
    me = lax.axis_index("row") * columns + lax.axis_index("col")
    enter(me, rows, columns)

    def copy(k):
        peer = lax.rem(me + k, count)
        return pltpu.make_async_remote_copy(
            src_ref=send_ref.at[peer],
            dst_ref=recv_ref.at[me],
            send_sem=send_sem.at[k],
            recv_sem=recv_sem.at[k],
            device_id=coordinates(peer, columns),
            device_id_type=MESH,
        )

    def arrival(k):
        source = lax.rem(me + count - k, count)
        return pltpu.make_async_remote_copy(
            src_ref=send_ref.at[source],
            dst_ref=recv_ref.at[source],
            send_sem=send_sem.at[k],
            recv_sem=recv_sem.at[k],
            device_id=coordinates(source, columns),
            device_id_type=MESH,
        )

    @pl.loop(1, count)
    def _(k):
        copy(k).start()

    recv_ref[me] = send_ref[me]

    @pl.loop(1, count)
    def _(k):
        arrival(k).wait_recv()

    @pl.loop(1, count)
    def _(k):
        copy(k).wait_send()


def exchange(send, rows, columns, collective_id):
    count = rows * columns
    return pl.pallas_call(
        functools.partial(exchange_kernel, rows, columns),
        out_shape=jax.ShapeDtypeStruct(send.shape, send.dtype),
        in_specs=[VMEM],
        out_specs=VMEM,
        scratch_shapes=[
            pltpu.SemaphoreType.DMA((count,)),
            pltpu.SemaphoreType.DMA((count,)),
        ],
        compiler_params=pltpu.CompilerParams(
            collective_id=collective_id, has_side_effects=True, vmem_limit_bytes=LIMIT
        ),
    )(send)


def spread_densities(rows, columns, own_ref, all_ref, left_ref, right_ref, send_sem, recv_sem):
    row, column = lax.axis_index("row"), lax.axis_index("col")
    count = rows * columns
    me = row * columns + column
    halo = left_ref.shape[0]
    blocks = own_ref.shape[0]
    after = coordinates(lax.rem(me + 1, count), columns)
    before = coordinates(lax.rem(me + count - 1, count), columns)
    halos = [
        pltpu.make_async_remote_copy(
            src_ref=own_ref.at[pl.ds(blocks - halo, halo)],
            dst_ref=left_ref,
            send_sem=send_sem.at[0],
            recv_sem=recv_sem.at[0],
            device_id=after,
            device_id_type=MESH,
        ),
        pltpu.make_async_remote_copy(
            src_ref=own_ref.at[pl.ds(0, halo)],
            dst_ref=right_ref,
            send_sem=send_sem.at[rows],
            recv_sem=recv_sem.at[rows],
            device_id=before,
            device_id_type=MESH,
        ),
    ]
    for copy in halos:
        copy.start()
    copies = []
    for k in range(1, rows):
        copies.append(
            pltpu.make_async_remote_copy(
                src_ref=own_ref,
                dst_ref=all_ref.at[row],
                send_sem=send_sem.at[k],
                recv_sem=recv_sem.at[k],
                device_id=(lax.rem(row + k, rows), column),
                device_id_type=MESH,
            )
        )
        copies[-1].start()
    all_ref[row] = own_ref[...]
    for copy in halos:
        copy.wait()
    for k in range(1, rows):
        source = lax.rem(row + rows - k, rows)
        pltpu.make_async_remote_copy(
            src_ref=own_ref,
            dst_ref=all_ref.at[source],
            send_sem=send_sem.at[k],
            recv_sem=recv_sem.at[k],
            device_id=(source, column),
            device_id_type=MESH,
        ).wait_recv()
    for copy in copies:
        copy.wait_send()


def spread_kernel(rows, columns, own_ref, all_ref, left_ref, right_ref, send_sem, recv_sem):
    enter(lax.axis_index("row") * columns + lax.axis_index("col"), rows, columns)
    spread_densities(rows, columns, own_ref, all_ref, left_ref, right_ref, send_sem, recv_sem)


def density_shapes(blocks, width, rows):
    halo = blocks // 4
    return [
        jax.ShapeDtypeStruct((rows, blocks, width), jnp.bfloat16),
        jax.ShapeDtypeStruct((halo, width), jnp.bfloat16),
        jax.ShapeDtypeStruct((halo, width), jnp.bfloat16),
    ]


def spread(own, rows, columns, collective_id):
    return pl.pallas_call(
        functools.partial(spread_kernel, rows, columns),
        out_shape=density_shapes(own.shape[0], own.shape[1], rows),
        in_specs=[VMEM],
        out_specs=[VMEM] * 3,
        scratch_shapes=[
            pltpu.SemaphoreType.DMA((rows + 1,)),
            pltpu.SemaphoreType.DMA((rows + 1,)),
        ],
        compiler_params=pltpu.CompilerParams(
            collective_id=collective_id, has_side_effects=True, vmem_limit_bytes=LIMIT
        ),
    )(own)


def split_dot(picker, value):
    high = value.astype(jnp.bfloat16)
    rest = value - high.astype(jnp.float32)
    middle = rest.astype(jnp.bfloat16)
    low = (rest - middle.astype(jnp.float32)).astype(jnp.bfloat16)
    dot = functools.partial(jnp.dot, picker, preferred_element_type=jnp.float32)
    return dot(high) + (dot(middle) + dot(low))


def one_hot(condition):
    return jnp.where(condition, 1.0, 0.0).astype(jnp.bfloat16)


def operator_kernel(
    sides,
    own_ref,
    all_ref,
    left_ref,
    right_ref,
    near_column_ref,
    near_row_ref,
    far_column_ref,
    far_row_ref,
    owner_ref,
    near_ref,
    far_left_ref,
    far_right_ref,
    image_ref,
    partial_ref,
    extended,
    near_picked,
    near_out,
    far_picked,
    far_out,
):
    step = pl.program_id(0)
    blocks = own_ref.shape[0]
    halo = left_ref.shape[0]
    rows = all_ref.shape[0]
    near_count = near_ref.shape[0]
    far_count = far_left_ref.shape[0]
    rank = far_left_ref.shape[1]
    width = sides * LANES
    nt = (((1,), (1,)), ((), ()))

    @pl.when(step == 0)
    def _():
        extended[0:halo] = left_ref[...]
        extended[halo : halo + blocks] = own_ref[...]
        extended[halo + blocks :] = right_ref[...]
        image_ref[...] = 0.5 * own_ref[...].astype(jnp.float32)

    reach = blocks + 2 * halo
    pick = one_hot(
        near_column_ref[...] == lax.broadcasted_iota(jnp.int32, (near_count, reach), 1)
    )
    near_picked[...] = jnp.dot(pick, extended[...], preferred_element_type=jnp.float32)
    batch = 8
    row_id = lax.rem(lax.broadcasted_iota(jnp.int32, (sides * batch, LANES), 0), batch)
    for j in range(near_count // batch):
        here = slice(j * batch, (j + 1) * batch)
        stacked = jnp.concatenate(
            [near_picked[here, s * LANES : (s + 1) * LANES] for s in range(sides)], axis=0
        ).astype(jnp.bfloat16)
        product = lax.dot_general(
            stacked,
            near_ref[here].reshape(batch * LANES, LANES),
            nt,
            preferred_element_type=jnp.float32,
        )
        value = jnp.zeros((sides * batch, LANES), jnp.float32)
        for e in range(batch):
            value = jnp.where(row_id == e, product[:, e * LANES : (e + 1) * LANES], value)
        for s in range(sides):
            near_out[here, s * LANES : (s + 1) * LANES] = value[s * batch : (s + 1) * batch]
    place = one_hot(
        near_row_ref[0] == lax.broadcasted_iota(jnp.int32, (blocks, near_count), 0)
    )
    image_ref[...] += split_dot(place, near_out[...])

    pick = one_hot(
        far_column_ref[...] == lax.broadcasted_iota(jnp.int32, (far_count, rows * blocks), 1)
    )
    far_picked[...] = jnp.dot(
        pick, all_ref[...].reshape(rows * blocks, width), preferred_element_type=jnp.float32
    )
    batch = 32
    row_id = lax.rem(lax.broadcasted_iota(jnp.int32, (sides * batch, batch * rank), 0), batch)
    for j in range(far_count // batch):
        here = slice(j * batch, (j + 1) * batch)
        stacked = jnp.concatenate(
            [far_picked[here, s * LANES : (s + 1) * LANES] for s in range(sides)], axis=0
        ).astype(jnp.bfloat16)
        product = lax.dot_general(
            stacked,
            far_right_ref[here].reshape(batch * rank, LANES),
            nt,
            preferred_element_type=jnp.float32,
        )
        coefficients = jnp.where(row_id == owner_ref[0, j : j + 1], product, 0.0).astype(
            jnp.bfloat16
        )
        value = jnp.dot(
            coefficients,
            far_left_ref[here].reshape(batch * rank, LANES),
            preferred_element_type=jnp.float32,
        )
        for s in range(sides):
            far_out[here, s * LANES : (s + 1) * LANES] = value[s * batch : (s + 1) * batch]
    place = one_hot(far_row_ref[0] == lax.broadcasted_iota(jnp.int32, (blocks, far_count), 0))
    partial_ref[0] = split_dot(place, far_out[...])


def operate(densities, own, tables, near_blocks, far_left, far_right, sides, groups):
    everything, left, right = densities
    near_column, near_row, far_column, far_row, owner = tables
    blocks, width = own.shape
    near_count = near_blocks.shape[0] // groups
    far_count = far_left.shape[0] // groups
    rank = far_left.shape[1]
    chunks = owner.shape[1]
    return pl.pallas_call(
        functools.partial(operator_kernel, sides),
        grid=(groups,),
        out_shape=[
            jax.ShapeDtypeStruct((blocks, width), jnp.float32),
            jax.ShapeDtypeStruct((groups, blocks, width), jnp.float32),
        ],
        in_specs=[
            VMEM,
            VMEM,
            VMEM,
            VMEM,
            pl.BlockSpec((near_count, 1), lambda i: (i, 0)),
            pl.BlockSpec((1, 1, near_count), lambda i: (i, 0, 0)),
            pl.BlockSpec((far_count, 1), lambda i: (i, 0)),
            pl.BlockSpec((1, 1, far_count), lambda i: (i, 0, 0)),
            pl.BlockSpec((1, chunks, owner.shape[2]), lambda i: (i, 0, 0)),
            pl.BlockSpec((near_count, LANES, LANES), lambda i: (i, 0, 0)),
            pl.BlockSpec((far_count, rank, LANES), lambda i: (i, 0, 0)),
            pl.BlockSpec((far_count, rank, LANES), lambda i: (i, 0, 0)),
        ],
        out_specs=[
            pl.BlockSpec((blocks, width), lambda i: (0, 0)),
            pl.BlockSpec((1, blocks, width), lambda i: (i, 0, 0)),
        ],
        scratch_shapes=[
            pltpu.VMEM((blocks + 2 * left.shape[0], width), jnp.bfloat16),
            pltpu.VMEM((near_count, width), jnp.float32),
            pltpu.VMEM((near_count, width), jnp.float32),
            pltpu.VMEM((far_count, width), jnp.float32),
            pltpu.VMEM((far_count, width), jnp.float32),
        ],
        compiler_params=pltpu.CompilerParams(vmem_limit_bytes=LIMIT),
    )(
        own,
        everything,
        left,
        right,
        near_column,
        near_row,
        far_column,
        far_row,
        owner,
        near_blocks,
        far_left,
        far_right,
    )


def collect_image(rows, columns, far_ref, near_ref, landed, image, send_sem, recv_sem):
    row, column = lax.axis_index("row"), lax.axis_index("col")
    copies = []
    for k in range(1, columns):
        peer = lax.rem(column + k, columns)
        copies.append(
            pltpu.make_async_remote_copy(
                src_ref=far_ref.at[peer],
                dst_ref=landed.at[column],
                send_sem=send_sem.at[k],
                recv_sem=recv_sem.at[k],
                device_id=(row, peer),
                device_id_type=MESH,
            )
        )
        copies[-1].start()
    image[...] = near_ref[...] + far_ref[column]
    for k in range(1, columns):
        source = lax.rem(column + columns - k, columns)
        pltpu.make_async_remote_copy(
            src_ref=far_ref.at[source],
            dst_ref=landed.at[source],
            send_sem=send_sem.at[k],
            recv_sem=recv_sem.at[k],
            device_id=(row, source),
            device_id_type=MESH,
        ).wait_recv()
        image[...] += landed[source]
    for copy in copies:
        copy.wait_send()


def all_sum(rows, columns, pairs, mine, parts, send_sem, recv_sem):
    count = rows * columns
    me = lax.axis_index("row") * columns + lax.axis_index("col")
    mine[...] = jnp.zeros(mine.shape, jnp.float32)
    place = 0
    for left, right in pairs:
        for s in range(left.shape[1] // LANES):
            here = slice(s * LANES, (s + 1) * LANES)
            mine[place : place + 1] = jnp.sum(left[:, here] * right[:, here], axis=0, keepdims=True)
            place += 1

    def copy(k, slot, peer):
        return pltpu.make_async_remote_copy(
            src_ref=mine,
            dst_ref=parts.at[slot],
            send_sem=send_sem.at[k],
            recv_sem=recv_sem.at[k],
            device_id=coordinates(peer, columns),
            device_id_type=MESH,
        )

    @pl.loop(1, count)
    def _(k):
        copy(k, me, lax.rem(me + k, count)).start()

    parts[me] = mine[...]

    @pl.loop(1, count)
    def _(k):
        source = lax.rem(me + count - k, count)
        copy(k, source, source).wait_recv()

    @pl.loop(1, count)
    def _(k):
        copy(k, me, lax.rem(me + k, count)).wait_send()

    return jnp.sum(jnp.sum(parts[...], axis=0), axis=1, keepdims=True)


def middle_kernel(
    rows,
    columns,
    far_ref,
    near_ref,
    first_ref,
    basis_ref,
    own_ref,
    all_ref,
    left_ref,
    right_ref,
    entries_ref,
    landed,
    image,
    mine,
    parts,
    mine_two,
    parts_two,
    collect_send,
    collect_recv,
    sum_send,
    sum_recv,
    sum_send_two,
    sum_recv_two,
    spread_send,
    spread_recv,
):
    me = lax.axis_index("row") * columns + lax.axis_index("col")
    panels = rows * columns * image.shape[0] * LANES
    sides = image.shape[1] // LANES
    lanes = [slice(s * LANES, (s + 1) * LANES) for s in range(sides)]
    enter(me, rows, columns)
    collect_image(rows, columns, far_ref, near_ref, landed, image, collect_send, collect_recv)
    project = (
        all_sum(rows, columns, [(first_ref, image)], mine, parts, sum_send, sum_recv) / panels
    )
    for s in range(sides):
        image[:, lanes[s]] = image[:, lanes[s]] - project[s : s + 1] * first_ref[:, lanes[s]]
    norm = jnp.sqrt(
        all_sum(
            rows, columns, [(image, image)], mine_two, parts_two, sum_send_two, sum_recv_two
        )
        / panels
        + epsilon
    )
    for s in range(sides):
        value = image[:, lanes[s]] / norm[s : s + 1]
        basis_ref[:, lanes[s]] = value
        own_ref[:, lanes[s]] = value.astype(jnp.bfloat16)
    entries_ref[0] = jnp.broadcast_to(project, mine.shape)
    entries_ref[1] = jnp.broadcast_to(norm, mine.shape)
    spread_densities(rows, columns, own_ref, all_ref, left_ref, right_ref, spread_send, spread_recv)


def middle(far, near, first, rows, columns, collective_id):
    blocks, width = near.shape
    count = rows * columns
    dma = pltpu.SemaphoreType.DMA
    return pl.pallas_call(
        functools.partial(middle_kernel, rows, columns),
        out_shape=[
            jax.ShapeDtypeStruct(near.shape, jnp.float32),
            jax.ShapeDtypeStruct(near.shape, jnp.bfloat16),
            *density_shapes(blocks, width, rows),
            jax.ShapeDtypeStruct((2, 8, LANES), jnp.float32),
        ],
        in_specs=[VMEM] * 3,
        out_specs=[VMEM] * 6,
        scratch_shapes=[
            pltpu.VMEM((columns, blocks, width), jnp.float32),
            pltpu.VMEM((blocks, width), jnp.float32),
            pltpu.VMEM((8, LANES), jnp.float32),
            pltpu.VMEM((count, 8, LANES), jnp.float32),
            pltpu.VMEM((8, LANES), jnp.float32),
            pltpu.VMEM((count, 8, LANES), jnp.float32),
            dma((columns,)),
            dma((columns,)),
            dma((count,)),
            dma((count,)),
            dma((count,)),
            dma((count,)),
            dma((rows + 1,)),
            dma((rows + 1,)),
        ],
        compiler_params=pltpu.CompilerParams(
            collective_id=collective_id, has_side_effects=True, vmem_limit_bytes=LIMIT
        ),
    )(far, near, first)


def last_kernel(
    rows,
    columns,
    far_ref,
    near_ref,
    first_ref,
    basis_ref,
    next_ref,
    entries_ref,
    landed,
    image,
    mine,
    parts,
    collect_send,
    collect_recv,
    sum_send,
    sum_recv,
):
    me = lax.axis_index("row") * columns + lax.axis_index("col")
    panels = rows * columns * image.shape[0] * LANES
    sides = image.shape[1] // LANES
    enter(me, rows, columns)
    collect_image(rows, columns, far_ref, near_ref, landed, image, collect_send, collect_recv)
    project = (
        all_sum(
            rows,
            columns,
            [(first_ref, image), (basis_ref, image)],
            mine,
            parts,
            sum_send,
            sum_recv,
        )
        / panels
    )
    for s in range(sides):
        here = slice(s * LANES, (s + 1) * LANES)
        next_ref[:, here] = (
            image[:, here]
            - project[s : s + 1] * first_ref[:, here]
            - project[sides + s : sides + s + 1] * basis_ref[:, here]
        )
    entries_ref[...] = jnp.broadcast_to(project, mine.shape)


def last(far, near, first, basis, rows, columns, collective_id):
    blocks, width = near.shape
    count = rows * columns
    dma = pltpu.SemaphoreType.DMA
    return pl.pallas_call(
        functools.partial(last_kernel, rows, columns),
        out_shape=[
            jax.ShapeDtypeStruct(near.shape, jnp.float32),
            jax.ShapeDtypeStruct((8, LANES), jnp.float32),
        ],
        in_specs=[VMEM] * 4,
        out_specs=[VMEM] * 2,
        scratch_shapes=[
            pltpu.VMEM((columns, blocks, width), jnp.float32),
            pltpu.VMEM((blocks, width), jnp.float32),
            pltpu.VMEM((8, LANES), jnp.float32),
            pltpu.VMEM((count, 8, LANES), jnp.float32),
            dma((columns,)),
            dma((columns,)),
            dma((count,)),
            dma((count,)),
        ],
        compiler_params=pltpu.CompilerParams(
            collective_id=collective_id, has_side_effects=True, vmem_limit_bytes=LIMIT
        ),
    )(far, near, first, basis)


def body(
    right_side,
    cluster_of,
    near_rows,
    near_columns,
    near_blocks,
    far_rows,
    far_columns,
    far_rank,
    far_left,
    far_right,
):
    rows = lax.axis_size("row")
    columns = lax.axis_size("col")
    count = rows * columns
    blocks, sides, lanes = right_side.shape
    width = sides * lanes
    capacity = 2 * blocks // count
    panels = blocks * count * lanes
    rank = far_left.shape[1]
    far_count = far_rows.shape[0] // columns
    near_count = near_rows.shape[0] // columns
    chunk = 32

    target = cluster_of // blocks
    place = cluster_of % blocks
    order = jnp.arange(blocks, dtype=jnp.int32)
    earlier = (target[None, :] == target[:, None]) & (order[None, :] < order[:, None])
    slot = target * capacity + jnp.sum(earlier.astype(jnp.int32), axis=1)
    slots = count * capacity
    to_slot = slot[None, :] == jnp.arange(slots, dtype=jnp.int32)[:, None]
    to_slot_f = to_slot.astype(jnp.float32)
    marks = jnp.sum(jnp.where(to_slot, place[None, :] + 1, 0), axis=1).astype(jnp.float32)

    lane = jnp.arange(lanes, dtype=jnp.int32)
    squares = jnp.sum(right_side * right_side, axis=(0, 2))
    half = lanes // 2
    step = half // sides
    square_lanes = jnp.repeat(squares, step)
    extra = jnp.concatenate(
        [
            jnp.broadcast_to(marks[:, None], (slots, half)),
            jnp.broadcast_to(square_lanes[None, :], (slots, half)),
        ],
        axis=1,
    )
    outgoing = jnp.dot(to_slot_f, right_side.reshape(blocks, width), precision=HIGH)
    arrived = exchange(
        jnp.concatenate([outgoing, extra], axis=1).reshape(count, capacity, width + lanes),
        rows,
        columns,
        0,
    )
    total = jnp.sum(arrived[:, 0, width + half :], axis=0).reshape(sides, step)[:, 0]
    side_norm = jnp.sqrt(total / panels + epsilon)
    arrived = arrived.reshape(slots, width + lanes)
    held = arrived[:, width].astype(jnp.int32) - 1
    from_slot = held[None, :] == order[:, None]
    to_cluster = from_slot.astype(jnp.float32)
    norm_lanes = jnp.repeat(side_norm, lanes)
    first = jnp.dot(to_cluster, arrived[:, :width], precision=HIGH) / norm_lanes[None, :]

    group = jnp.arange(columns, dtype=jnp.int32)[:, None]
    entry_rank = jnp.arange(rank, dtype=jnp.int32)
    owner = jnp.where(
        entry_rank[None, :] < far_rank[:, None],
        (jnp.arange(far_rank.shape[0], dtype=jnp.int32) % chunk)[:, None],
        -1,
    ).reshape(columns, far_count // chunk, chunk * rank)
    tables = (
        near_columns[:, None],
        near_rows.reshape(columns, 1, near_count),
        far_columns[:, None],
        (far_rows.reshape(columns, far_count) - group * blocks).reshape(columns, 1, far_count),
        owner,
    )
    own = first.astype(jnp.bfloat16)
    densities = spread(own, rows, columns, 1)
    near, far = operate(densities, own, tables, near_blocks, far_left, far_right, sides, columns)
    basis, own, *densities, entries = middle(far, near, first, rows, columns, 2)
    near, far = operate(densities, own, tables, near_blocks, far_left, far_right, sides, columns)
    following, entries_two = last(far, near, first, basis, rows, columns, 3)

    results = jnp.concatenate([basis, following], axis=1)
    returned = exchange(
        jnp.dot(to_cluster.T, results, precision=HIGH).reshape(count, capacity, 2 * width),
        rows,
        columns,
        4,
    )
    results = jnp.dot(to_slot_f.T, returned.reshape(slots, 2 * width), precision=HIGH)
    second_basis = results[:, :width].reshape(blocks, sides, lanes)
    next_vector = results[:, width:].reshape(blocks, sides, lanes)
    hessenberg = jnp.concatenate(
        [
            side_norm[None, :],
            entries[:, :sides, 0],
            entries_two[: 2 * sides, 0].reshape(2, sides),
        ],
        axis=0,
    )
    return (second_basis, next_vector, hessenberg)


def solution(mesh):
    vector = P(("row", "col"), None, None)
    table = P(("row", "col"))
    placed = (vector, table, table, table, vector, table, table, table, vector, vector)
    return jax.shard_map(
        body,
        mesh=mesh,
        in_specs=placed,
        out_specs=(vector, vector, P()),
        check_vma=False,
    )
```

```python
import functools

import jax
import jax.numpy as jnp
from jax import lax
from jax.experimental import pallas as pl
from jax.experimental.pallas import tpu as pltpu
from jax.sharding import PartitionSpec as P

epsilon = 1e-06
MESH = pl.DeviceIdType.MESH
HIGH = lax.Precision.HIGHEST
VMEM = pl.BlockSpec(memory_space=pltpu.VMEM)
LANES = 128
LIMIT = 56 * 2**20


def coordinates(index, column_count):
    return (lax.div(index, column_count), lax.rem(index, column_count))


def enter(me, rows, columns):
    count = rows * columns
    barrier = pltpu.get_barrier_semaphore()

    @pl.loop(1, count)
    def _(k):
        pl.semaphore_signal(
            barrier,
            inc=1,
            device_id=coordinates(lax.rem(me + k, count), columns),
            device_id_type=MESH,
        )

    pl.semaphore_wait(barrier, count - 1)


def exchange_kernel(rows, columns, send_ref, recv_ref, send_sem, recv_sem):
    count = rows * columns
    me = lax.axis_index("row") * columns + lax.axis_index("col")
    enter(me, rows, columns)

    def copy(k):
        peer = lax.rem(me + k, count)
        return pltpu.make_async_remote_copy(
            src_ref=send_ref.at[peer],
            dst_ref=recv_ref.at[me],
            send_sem=send_sem.at[k],
            recv_sem=recv_sem.at[k],
            device_id=coordinates(peer, columns),
            device_id_type=MESH,
        )

    def arrival(k):
        source = lax.rem(me + count - k, count)
        return pltpu.make_async_remote_copy(
            src_ref=send_ref.at[source],
            dst_ref=recv_ref.at[source],
            send_sem=send_sem.at[k],
            recv_sem=recv_sem.at[k],
            device_id=coordinates(source, columns),
            device_id_type=MESH,
        )

    @pl.loop(1, count)
    def _(k):
        copy(k).start()

    recv_ref[me] = send_ref[me]

    @pl.loop(1, count)
    def _(k):
        arrival(k).wait_recv()

    @pl.loop(1, count)
    def _(k):
        copy(k).wait_send()


def exchange(send, rows, columns, collective_id):
    count = rows * columns
    return pl.pallas_call(
        functools.partial(exchange_kernel, rows, columns),
        out_shape=jax.ShapeDtypeStruct(send.shape, send.dtype),
        in_specs=[VMEM],
        out_specs=VMEM,
        scratch_shapes=[
            pltpu.SemaphoreType.DMA((count,)),
            pltpu.SemaphoreType.DMA((count,)),
        ],
        compiler_params=pltpu.CompilerParams(
            collective_id=collective_id, has_side_effects=True, vmem_limit_bytes=LIMIT
        ),
    )(send)


def split_dot(picker, value):
    high = value.astype(jnp.bfloat16)
    rest = value - high.astype(jnp.float32)
    middle = rest.astype(jnp.bfloat16)
    low = (rest - middle.astype(jnp.float32)).astype(jnp.bfloat16)
    dot = functools.partial(jnp.dot, picker, preferred_element_type=jnp.float32)
    return dot(high) + (dot(middle) + dot(low))


def one_hot(condition):
    return jnp.where(condition, 1.0, 0.0).astype(jnp.bfloat16)


def remote(source, destination, sends, recvs, k, device):
    return pltpu.make_async_remote_copy(
        src_ref=source,
        dst_ref=destination,
        send_sem=sends.at[k],
        recv_sem=recvs.at[k],
        device_id=device,
        device_id_type=MESH,
    )


def near_group(sides, g, tables_ref, extended, near_ref, near_out, image):
    near_count = near_ref.shape[1]
    reach = extended.shape[0]
    blocks = image.shape[0]
    table = tables_ref[g]
    turned = table.T
    column = turned[:near_count, 0:1]
    pick = one_hot(
        column == lax.broadcasted_iota(jnp.int32, (near_count, reach), 1).astype(jnp.float32)
    )
    picked = jnp.dot(pick, extended[...], preferred_element_type=jnp.float32)
    batch = 8
    row_id = lax.rem(lax.broadcasted_iota(jnp.int32, (sides * batch, LANES), 0), batch)
    for j in range(near_count // batch):
        here = slice(j * batch, (j + 1) * batch)
        stacked = jnp.concatenate(
            [picked[here, s * LANES : (s + 1) * LANES] for s in range(sides)], axis=0
        ).astype(jnp.bfloat16)
        product = lax.dot_general(
            stacked,
            near_ref[g, here].reshape(batch * LANES, LANES),
            (((1,), (1,)), ((), ())),
            preferred_element_type=jnp.float32,
        )
        value = jnp.zeros((sides * batch, LANES), jnp.float32)
        for e in range(batch):
            value = jnp.where(row_id == e, product[:, e * LANES : (e + 1) * LANES], value)
        for s in range(sides):
            near_out[here, s * LANES : (s + 1) * LANES] = value[s * batch : (s + 1) * batch]
    place = one_hot(
        table[1:2, :near_count]
        == lax.broadcasted_iota(jnp.int32, (blocks, near_count), 0).astype(jnp.float32)
    )
    image[...] += split_dot(place, near_out[...])


def far_group(sides, g, tables_ref, everything, far_left, far_right, far_out):
    rows, blocks, width = everything.shape
    far_count, rank = far_left.shape[1:3]
    table = tables_ref[g]
    turned = table.T
    lanes = lax.broadcasted_iota(jnp.int32, (far_count, rows * blocks), 1).astype(jnp.float32)
    pick = one_hot(turned[:far_count, 2:3] == lanes)
    picked = jnp.dot(
        pick, everything[...].reshape(rows * blocks, width), preferred_element_type=jnp.float32
    )
    batch = 32
    shape = (sides * batch, batch * rank)
    entry = lax.rem(lax.broadcasted_iota(jnp.int32, shape, 0), batch)
    lane = lax.broadcasted_iota(jnp.int32, shape, 1)
    term = lax.rem(lane, rank).astype(jnp.float32)
    own_entry = lax.div(lane, rank) == entry
    for j in range(far_count // batch):
        here = slice(j * batch, (j + 1) * batch)
        stacked = jnp.concatenate(
            [picked[here, s * LANES : (s + 1) * LANES] for s in range(sides)], axis=0
        ).astype(jnp.bfloat16)
        product = lax.dot_general(
            stacked,
            far_right[g, here].reshape(batch * rank, LANES),
            (((1,), (1,)), ((), ())),
            preferred_element_type=jnp.float32,
        )
        ranks = jnp.concatenate([turned[here, 4:5]] * sides, axis=0)
        coefficients = jnp.where(own_entry & (term < ranks), product, 0.0).astype(jnp.bfloat16)
        value = jnp.dot(
            coefficients,
            far_left[g, here].reshape(batch * rank, LANES),
            preferred_element_type=jnp.float32,
        )
        for s in range(sides):
            far_out[here, s * LANES : (s + 1) * LANES] = value[s * batch : (s + 1) * batch]
    place = one_hot(
        table[3:4, :far_count]
        == lax.broadcasted_iota(jnp.int32, (blocks, far_count), 0).astype(jnp.float32)
    )
    return split_dot(place, far_out[...])


def arnoldi_kernel(
    rows,
    columns,
    first_ref,
    tables_ref,
    to_mesh_ref,
    near_hbm,
    far_left_hbm,
    far_right_hbm,
    basis_back_ref,
    image_back_ref,
    entries_ref,
    entries_two_ref,
    near_ref,
    far_left,
    far_right,
    own,
    basis,
    image,
    everything,
    extended,
    left,
    right,
    near_out,
    far_out,
    to_partner,
    from_partner,
    to_chips,
    from_chips,
    outgoing,
    outgoing_two,
    mine,
    parts,
    load_sem,
    halo_send,
    halo_recv,
    spread_send,
    spread_recv,
    pair_send,
    pair_recv,
    chip_send,
    chip_recv,
    sum_send,
    sum_recv,
    back_send,
    back_recv,
):
    row, column = lax.axis_index("row"), lax.axis_index("col")
    count = rows * columns
    me = row * columns + column
    blocks, width = first_ref.shape
    sides = width // LANES
    halo = left.shape[0]
    groups = near_ref.shape[0]
    pairs = columns // 2
    chip, core = lax.div(column, 2), lax.rem(column, 2)
    partner = 2 * chip + 1 - core
    panels = count * blocks * LANES
    lanes = [slice(s * LANES, (s + 1) * LANES) for s in range(sides)]
    capacity = outgoing.shape[1]

    def load(kind, g):
        source, target = (
            (near_hbm, near_ref),
            (far_left_hbm, far_left),
            (far_right_hbm, far_right),
        )[kind]
        return pltpu.make_async_copy(source.at[g], target.at[g], load_sem.at[kind, g])

    for kind in range(3):

        @pl.loop(0, groups)
        def _(g, kind=kind):
            load(kind, g).start()

    enter(me, rows, columns)

    def operate(a, between):
        after = coordinates(lax.rem(me + 1, count), columns)
        before = coordinates(lax.rem(me + count - 1, count), columns)
        halos = [
            remote(
                own.at[pl.ds(blocks - halo, halo)],
                left,
                halo_send.at[a],
                halo_recv.at[a],
                0,
                after,
            ),
            remote(own.at[pl.ds(0, halo)], right, halo_send.at[a], halo_recv.at[a], 1, before),
        ]
        for copy in halos:
            copy.start()
        copies = [
            remote(
                own,
                everything.at[row],
                spread_send.at[a],
                spread_recv.at[a],
                k,
                (lax.rem(row + k, rows), column),
            )
            for k in range(1, rows)
        ]
        for copy in copies:
            copy.start()
        everything[row] = own[...]
        image[...] = 0.5 * own[...].astype(jnp.float32)
        extended[halo : halo + blocks] = own[...]
        for copy in halos:
            copy.wait()
        extended[0:halo] = left[...]
        extended[halo + blocks :] = right[...]

        @pl.loop(0, groups)
        def _(g):
            if a == 0:
                load(0, g).wait()
            near_group(sides, g, tables_ref, extended, near_ref, near_out, image)

        for k in range(1, rows):
            source = lax.rem(row + rows - k, rows)
            remote(
                own,
                everything.at[source],
                spread_send.at[a],
                spread_recv.at[a],
                k,
                (source, column),
            ).wait_recv()
        for copy in copies:
            copy.wait_send()
        between()
        if a == 0:
            for kind in (1, 2):

                @pl.loop(0, groups)
                def _(g, kind=kind):
                    load(kind, g).wait()

        far = functools.partial(
            far_group,
            sides,
            tables_ref=tables_ref,
            everything=everything,
            far_left=far_left,
            far_right=far_right,
            far_out=far_out,
        )

        def pair_copy(k, q):
            return remote(
                to_partner.at[q],
                from_partner.at[q],
                pair_send.at[a],
                pair_recv.at[a],
                k,
                (row, partner),
            )

        def chip_copy(k, q):
            return remote(
                to_chips.at[q],
                from_chips.at[chip],
                chip_send.at[a],
                chip_recv.at[a],
                k,
                (row, 2 * q + core),
            )

        @pl.loop(1, pairs + 1)
        def _(i):
            q = lax.rem(chip + i, pairs)
            k = i - 1
            to_partner[q] = far(2 * q + 1 - core)
            pair_copy(k, q).start()
            to_chips[q] = far(2 * q + core)
            pair_copy(k, q).wait_recv()
            to_chips[q] = to_chips[q] + from_partner[q]

            @pl.when(i < pairs)
            def _():
                chip_copy(k, q).start()

        image[...] += to_chips[chip]
        for i in range(1, pairs):
            source = lax.rem(chip + pairs - i, pairs)
            remote(
                to_chips.at[source],
                from_chips.at[source],
                chip_send.at[a],
                chip_recv.at[a],
                i - 1,
                (row, 2 * source + core),
            ).wait_recv()
            image[...] += from_chips[source]
        for i in range(1, pairs + 1):
            q = lax.rem(chip + i, pairs)
            pair_copy(i - 1, q).wait_send()
            if i < pairs:
                chip_copy(i - 1, q).wait_send()

    def all_sum(n, pairings):
        place = 0
        mine[n] = jnp.zeros(mine.shape[1:], jnp.float32)
        for one, two in pairings:
            for here in lanes:
                mine[n, place : place + 1] = jnp.sum(
                    one[:, here] * two[:, here], axis=0, keepdims=True
                )
                place += 1

        def copy(k, slot, peer):
            return remote(
                mine.at[n],
                parts.at[n, slot],
                sum_send.at[n],
                sum_recv.at[n],
                k,
                coordinates(peer, columns),
            )

        @pl.loop(1, count)
        def _(k):
            copy(k, me, lax.rem(me + k, count)).start()

        parts[n, me] = mine[n]

        @pl.loop(1, count)
        def _(k):
            source = lax.rem(me + count - k, count)
            copy(k, source, source).wait_recv()

        @pl.loop(1, count)
        def _(k):
            copy(k, me, lax.rem(me + k, count)).wait_send()

        return jnp.sum(jnp.sum(parts[n], axis=0), axis=1, keepdims=True) / panels

    def back(n, sent, landed):
        def copy(k, peer, slot):
            return remote(
                sent.at[peer],
                landed.at[slot],
                back_send.at[n],
                back_recv.at[n],
                k,
                coordinates(peer, columns),
            )

        def start(value):
            picked = split_dot(to_mesh_ref[...], value[...])
            for d in range(count):
                sent[d] = picked[d * capacity : (d + 1) * capacity]

            @pl.loop(1, count)
            def _(k):
                copy(k, lax.rem(me + k, count), me).start()

            landed[me] = sent[me]

        def wait():
            @pl.loop(1, count)
            def _(k):
                source = lax.rem(me + count - k, count)
                copy(k, source, source).wait_recv()

            @pl.loop(1, count)
            def _(k):
                copy(k, lax.rem(me + k, count), me).wait_send()

        return start, wait

    basis_start, basis_wait = back(0, outgoing, basis_back_ref)
    image_start, image_wait = back(1, outgoing_two, image_back_ref)

    own[...] = first_ref[...].astype(jnp.bfloat16)
    operate(0, lambda: None)
    project = all_sum(0, [(first_ref, image)])
    for s in range(sides):
        image[:, lanes[s]] = image[:, lanes[s]] - project[s : s + 1] * first_ref[:, lanes[s]]
    norm = jnp.sqrt(all_sum(1, [(image, image)]) + epsilon)
    for s in range(sides):
        value = image[:, lanes[s]] / norm[s : s + 1]
        basis[:, lanes[s]] = value
        own[:, lanes[s]] = value.astype(jnp.bfloat16)
    entries_ref[0] = jnp.broadcast_to(project, mine.shape[1:])
    entries_ref[1] = jnp.broadcast_to(norm, mine.shape[1:])
    operate(1, lambda: basis_start(basis))
    image_start(image)
    projects = all_sum(2, [(first_ref, image), (basis, image)])
    entries_two_ref[...] = jnp.broadcast_to(projects, mine.shape[1:])
    basis_wait()
    image_wait()


def arnoldi(first, tables, to_mesh, near_blocks, far_left, far_right, rows, columns, capacity):
    blocks, width = first.shape
    count = rows * columns
    groups = columns
    near_blocks = near_blocks.reshape(groups, -1, *near_blocks.shape[1:])
    far_left = far_left.reshape(groups, -1, *far_left.shape[1:])
    far_right = far_right.reshape(groups, -1, *far_right.shape[1:])
    halo = blocks // 4
    pairs = columns // 2
    dma = pltpu.SemaphoreType.DMA
    real, half = jnp.float32, jnp.bfloat16
    slots = (count, capacity, width)
    hbm = pl.BlockSpec(memory_space=pl.ANY)
    return pl.pallas_call(
        functools.partial(arnoldi_kernel, rows, columns),
        out_shape=[
            jax.ShapeDtypeStruct(slots, real),
            jax.ShapeDtypeStruct(slots, real),
            jax.ShapeDtypeStruct((2, 8, LANES), real),
            jax.ShapeDtypeStruct((8, LANES), real),
        ],
        in_specs=[VMEM] * 3 + [hbm] * 3,
        out_specs=[VMEM] * 4,
        scratch_shapes=[
            pltpu.VMEM(near_blocks.shape, half),
            pltpu.VMEM(far_left.shape, half),
            pltpu.VMEM(far_right.shape, half),
            pltpu.VMEM((blocks, width), half),
            pltpu.VMEM((blocks, width), real),
            pltpu.VMEM((blocks, width), real),
            pltpu.VMEM((rows, blocks, width), half),
            pltpu.VMEM((blocks + 2 * halo, width), half),
            pltpu.VMEM((halo, width), half),
            pltpu.VMEM((halo, width), half),
            pltpu.VMEM((near_blocks.shape[1], width), real),
            pltpu.VMEM((far_left.shape[1], width), real),
            pltpu.VMEM((pairs, blocks, width), real),
            pltpu.VMEM((pairs, blocks, width), real),
            pltpu.VMEM((pairs, blocks, width), real),
            pltpu.VMEM((pairs, blocks, width), real),
            pltpu.VMEM(slots, real),
            pltpu.VMEM(slots, real),
            pltpu.VMEM((3, 8, LANES), real),
            pltpu.VMEM((3, count, 8, LANES), real),
            dma((3, groups)),
            dma((2, 2)),
            dma((2, 2)),
            dma((2, rows)),
            dma((2, rows)),
            dma((2, pairs)),
            dma((2, pairs)),
            dma((2, pairs)),
            dma((2, pairs)),
            dma((3, count)),
            dma((3, count)),
            dma((2, count)),
            dma((2, count)),
        ],
        compiler_params=pltpu.CompilerParams(
            collective_id=1, has_side_effects=True, vmem_limit_bytes=LIMIT
        ),
    )(first, tables, to_mesh, near_blocks, far_left, far_right)


def body(
    right_side,
    cluster_of,
    near_rows,
    near_columns,
    near_blocks,
    far_rows,
    far_columns,
    far_rank,
    far_left,
    far_right,
):
    rows = lax.axis_size("row")
    columns = lax.axis_size("col")
    count = rows * columns
    blocks, sides, lanes = right_side.shape
    width = sides * lanes
    capacity = 2 * blocks // count
    panels = blocks * count * lanes
    far_count = far_rows.shape[0] // columns

    target = cluster_of // blocks
    place = cluster_of % blocks
    order = jnp.arange(blocks, dtype=jnp.int32)
    earlier = (target[None, :] == target[:, None]) & (order[None, :] < order[:, None])
    slot = target * capacity + jnp.sum(earlier.astype(jnp.int32), axis=1)
    slots = count * capacity
    to_slot = slot[None, :] == jnp.arange(slots, dtype=jnp.int32)[:, None]
    to_slot_f = to_slot.astype(jnp.float32)
    marks = jnp.sum(jnp.where(to_slot, place[None, :] + 1, 0), axis=1).astype(jnp.float32)

    lane = jnp.arange(lanes, dtype=jnp.int32)
    squares = jnp.sum(right_side * right_side, axis=(0, 2))
    half = lanes // 2
    step = half // sides
    square_lanes = jnp.repeat(squares, step)
    extra = jnp.concatenate(
        [
            jnp.broadcast_to(marks[:, None], (slots, half)),
            jnp.broadcast_to(square_lanes[None, :], (slots, half)),
        ],
        axis=1,
    )
    outgoing = jnp.dot(to_slot_f, right_side.reshape(blocks, width), precision=HIGH)
    arrived = exchange(
        jnp.concatenate([outgoing, extra], axis=1).reshape(count, capacity, width + lanes),
        rows,
        columns,
        0,
    )
    total = jnp.sum(arrived[:, 0, width + half :], axis=0).reshape(sides, step)[:, 0]
    side_norm = jnp.sqrt(total / panels + epsilon)
    arrived = arrived.reshape(slots, width + lanes)
    held = arrived[:, width].astype(jnp.int32) - 1
    from_slot = held[None, :] == order[:, None]
    to_cluster = from_slot.astype(jnp.float32)
    norm_lanes = jnp.repeat(side_norm, lanes)
    first = jnp.dot(to_cluster, arrived[:, :width], precision=HIGH) / norm_lanes[None, :]


    group = jnp.arange(columns, dtype=jnp.int32)[:, None]

    def table(values):
        values = values.reshape(columns, -1)
        return jnp.pad(values, ((0, 0), (0, lanes - values.shape[1])))

    blank = jnp.zeros((columns, lanes), jnp.int32)
    tables = jnp.stack(
        [
            table(near_columns),
            table(near_rows),
            table(far_columns),
            table(far_rows.reshape(columns, far_count) - group * blocks),
            table(far_rank),
            blank,
            blank,
            blank,
        ],
        axis=1,
    ).astype(jnp.float32)
    to_mesh = (held[:, None] == order[None, :]).astype(jnp.bfloat16)
    basis_back, image_back, entries, entries_two = arnoldi(
        first, tables, to_mesh, near_blocks, far_left, far_right, rows, columns, capacity
    )
    local = to_slot_f.T
    project_two = jnp.repeat(entries_two[:sides, 0], lanes)
    project_three = jnp.repeat(entries_two[sides : 2 * sides, 0], lanes)
    basis = jnp.dot(local, basis_back.reshape(slots, width), precision=HIGH)
    image_two = jnp.dot(local, image_back.reshape(slots, width), precision=HIGH)
    mesh_first = right_side.reshape(blocks, width) / norm_lanes[None, :]
    following = image_two - project_two[None, :] * mesh_first - project_three[None, :] * basis
    second_basis = basis.reshape(blocks, sides, lanes)
    next_vector = following.reshape(blocks, sides, lanes)
    hessenberg = jnp.concatenate(
        [
            side_norm[None, :],
            entries[:, :sides, 0],
            entries_two[: 2 * sides, 0].reshape(2, sides),
        ],
        axis=0,
    )
    return (second_basis, next_vector, hessenberg)


def solution(mesh):
    vector = P(("row", "col"), None, None)
    table = P(("row", "col"))
    placed = (vector, table, table, table, vector, table, table, table, vector, vector)
    return jax.shard_map(
        body,
        mesh=mesh,
        in_specs=placed,
        out_specs=(vector, vector, P()),
        check_vma=False,
    )
```

```python
import functools

import jax
import jax.numpy as jnp
from jax import lax
from jax.experimental import pallas as pl
from jax.experimental.pallas import tpu as pltpu
from jax.sharding import PartitionSpec as P

epsilon = 1e-06
MESH = pl.DeviceIdType.MESH
HIGH = lax.Precision.HIGHEST
VMEM = pl.BlockSpec(memory_space=pltpu.VMEM)
LANES = 128
LIMIT = 56 * 2**20


def coordinates(index, column_count):
    return (lax.div(index, column_count), lax.rem(index, column_count))


def enter(me, rows, columns):
    count = rows * columns
    barrier = pltpu.get_barrier_semaphore()

    @pl.loop(1, count)
    def _(k):
        pl.semaphore_signal(
            barrier,
            inc=1,
            device_id=coordinates(lax.rem(me + k, count), columns),
            device_id_type=MESH,
        )

    pl.semaphore_wait(barrier, count - 1)


def exchange_kernel(rows, columns, send_ref, recv_ref, send_sem, recv_sem):
    count = rows * columns
    me = lax.axis_index("row") * columns + lax.axis_index("col")
    enter(me, rows, columns)

    def copy(k):
        peer = lax.rem(me + k, count)
        return pltpu.make_async_remote_copy(
            src_ref=send_ref.at[peer],
            dst_ref=recv_ref.at[me],
            send_sem=send_sem.at[k],
            recv_sem=recv_sem.at[k],
            device_id=coordinates(peer, columns),
            device_id_type=MESH,
        )

    def arrival(k):
        source = lax.rem(me + count - k, count)
        return pltpu.make_async_remote_copy(
            src_ref=send_ref.at[source],
            dst_ref=recv_ref.at[source],
            send_sem=send_sem.at[k],
            recv_sem=recv_sem.at[k],
            device_id=coordinates(source, columns),
            device_id_type=MESH,
        )

    @pl.loop(1, count)
    def _(k):
        copy(k).start()

    recv_ref[me] = send_ref[me]

    @pl.loop(1, count)
    def _(k):
        arrival(k).wait_recv()

    @pl.loop(1, count)
    def _(k):
        copy(k).wait_send()


def exchange(send, rows, columns, collective_id):
    count = rows * columns
    return pl.pallas_call(
        functools.partial(exchange_kernel, rows, columns),
        out_shape=jax.ShapeDtypeStruct(send.shape, send.dtype),
        in_specs=[VMEM],
        out_specs=VMEM,
        scratch_shapes=[
            pltpu.SemaphoreType.DMA((count,)),
            pltpu.SemaphoreType.DMA((count,)),
        ],
        compiler_params=pltpu.CompilerParams(
            collective_id=collective_id, has_side_effects=True, vmem_limit_bytes=LIMIT
        ),
    )(send)


def split_dot(picker, value):
    high = value.astype(jnp.bfloat16)
    rest = value - high.astype(jnp.float32)
    middle = rest.astype(jnp.bfloat16)
    low = (rest - middle.astype(jnp.float32)).astype(jnp.bfloat16)
    dot = functools.partial(jnp.dot, picker, preferred_element_type=jnp.float32)
    return dot(high) + (dot(middle) + dot(low))


def one_hot(condition):
    return jnp.where(condition, 1.0, 0.0).astype(jnp.bfloat16)


def remote(source, destination, sends, recvs, k, device):
    return pltpu.make_async_remote_copy(
        src_ref=source,
        dst_ref=destination,
        send_sem=sends.at[k],
        recv_sem=recvs.at[k],
        device_id=device,
        device_id_type=MESH,
    )


def near_group(sides, g, tables_ref, extended, near_ref, near_out, image):
    near_count = near_ref.shape[1]
    reach = extended.shape[0]
    blocks = image.shape[0]
    table = tables_ref[g]
    turned = table.T
    column = turned[:near_count, 0:1]
    pick = one_hot(
        column == lax.broadcasted_iota(jnp.int32, (near_count, reach), 1).astype(jnp.float32)
    )
    picked = jnp.dot(pick, extended[...], preferred_element_type=jnp.float32)
    batch = 8
    row_id = lax.rem(lax.broadcasted_iota(jnp.int32, (sides * batch, LANES), 0), batch)
    for j in range(near_count // batch):
        here = slice(j * batch, (j + 1) * batch)
        stacked = jnp.concatenate(
            [picked[here, s * LANES : (s + 1) * LANES] for s in range(sides)], axis=0
        ).astype(jnp.bfloat16)
        product = lax.dot_general(
            stacked,
            near_ref[g, here].reshape(batch * LANES, LANES),
            (((1,), (1,)), ((), ())),
            preferred_element_type=jnp.float32,
        )
        value = jnp.zeros((sides * batch, LANES), jnp.float32)
        for e in range(batch):
            value = jnp.where(row_id == e, product[:, e * LANES : (e + 1) * LANES], value)
        for s in range(sides):
            near_out[here, s * LANES : (s + 1) * LANES] = value[s * batch : (s + 1) * batch]
    place = one_hot(
        table[1:2, :near_count]
        == lax.broadcasted_iota(jnp.int32, (blocks, near_count), 0).astype(jnp.float32)
    )
    image[...] += split_dot(place, near_out[...])


def far_group(sides, g, tables_ref, everything, far_left, far_right, far_out):
    rows, blocks, width = everything.shape
    far_count, rank = far_left.shape[1:3]
    table = tables_ref[g]
    turned = table.T
    lanes = lax.broadcasted_iota(jnp.int32, (far_count, rows * blocks), 1).astype(jnp.float32)
    pick = one_hot(turned[:far_count, 2:3] == lanes)
    picked = jnp.dot(
        pick, everything[...].reshape(rows * blocks, width), preferred_element_type=jnp.float32
    )
    batch = 32
    shape = (sides * batch, batch * rank)
    entry = lax.rem(lax.broadcasted_iota(jnp.int32, shape, 0), batch)
    lane = lax.broadcasted_iota(jnp.int32, shape, 1)
    term = lax.rem(lane, rank).astype(jnp.float32)
    own_entry = lax.div(lane, rank) == entry
    for j in range(far_count // batch):
        here = slice(j * batch, (j + 1) * batch)
        stacked = jnp.concatenate(
            [picked[here, s * LANES : (s + 1) * LANES] for s in range(sides)], axis=0
        ).astype(jnp.bfloat16)
        product = lax.dot_general(
            stacked,
            far_right[g, here].reshape(batch * rank, LANES),
            (((1,), (1,)), ((), ())),
            preferred_element_type=jnp.float32,
        )
        ranks = jnp.concatenate([turned[here, 4:5]] * sides, axis=0)
        coefficients = jnp.where(own_entry & (term < ranks), product, 0.0).astype(jnp.bfloat16)
        value = jnp.dot(
            coefficients,
            far_left[g, here].reshape(batch * rank, LANES),
            preferred_element_type=jnp.float32,
        )
        for s in range(sides):
            far_out[here, s * LANES : (s + 1) * LANES] = value[s * batch : (s + 1) * batch]
    place = one_hot(
        table[3:4, :far_count]
        == lax.broadcasted_iota(jnp.int32, (blocks, far_count), 0).astype(jnp.float32)
    )
    return split_dot(place, far_out[...])


def arnoldi_kernel(
    rows,
    columns,
    first_ref,
    near_columns_ref,
    near_rows_ref,
    far_columns_ref,
    far_rows_ref,
    far_rank_ref,
    to_mesh_ref,
    to_own_ref,
    mesh_first_ref,
    near_hbm,
    far_left_hbm,
    far_right_hbm,
    basis_ref,
    next_ref,
    entries_ref,
    tables_ref,
    basis_back_ref,
    image_back_ref,
    flat,
    near_ref,
    far_left,
    far_right,
    own,
    basis,
    image,
    everything,
    extended,
    left,
    right,
    near_out,
    far_out,
    to_partner,
    from_partner,
    to_chips,
    from_chips,
    outgoing,
    outgoing_two,
    mine,
    parts,
    load_sem,
    halo_send,
    halo_recv,
    spread_send,
    spread_recv,
    pair_send,
    pair_recv,
    chip_send,
    chip_recv,
    sum_send,
    sum_recv,
    back_send,
    back_recv,
):
    row, column = lax.axis_index("row"), lax.axis_index("col")
    count = rows * columns
    me = row * columns + column
    blocks, width = first_ref.shape
    sides = width // LANES
    halo = left.shape[0]
    groups = near_ref.shape[0]
    pairs = columns // 2
    chip, core = lax.div(column, 2), lax.rem(column, 2)
    partner = 2 * chip + 1 - core
    panels = count * blocks * LANES
    lanes = [slice(s * LANES, (s + 1) * LANES) for s in range(sides)]
    capacity = outgoing.shape[1]

    def load(kind, g):
        source, target = (
            (near_hbm, near_ref),
            (far_left_hbm, far_left),
            (far_right_hbm, far_right),
        )[kind]
        return pltpu.make_async_copy(source.at[g], target.at[g], load_sem.at[kind, g])

    for kind in range(3):

        @pl.loop(0, groups)
        def _(g, kind=kind):
            load(kind, g).start()

    tables_ref[...] = jnp.zeros(tables_ref.shape, jnp.float32)
    for g in range(groups):
        for place, source in enumerate(
            (near_columns_ref, near_rows_ref, far_columns_ref, far_rows_ref, far_rank_ref)
        ):
            value = source[g : g + 1]
            if source is far_rows_ref:
                value = value - g * blocks
            tables_ref[g, place : place + 1, : source.shape[1]] = value.astype(jnp.float32)
    enter(me, rows, columns)

    def operate(a, between):
        after = coordinates(lax.rem(me + 1, count), columns)
        before = coordinates(lax.rem(me + count - 1, count), columns)
        halos = [
            remote(
                own.at[pl.ds(blocks - halo, halo)],
                left,
                halo_send.at[a],
                halo_recv.at[a],
                0,
                after,
            ),
            remote(own.at[pl.ds(0, halo)], right, halo_send.at[a], halo_recv.at[a], 1, before),
        ]
        for copy in halos:
            copy.start()
        everything[row] = own[...]

        def inside(index):
            return (index >= 0) & (index < rows)

        def hop(way, distance, slot):
            sign = 1 - 2 * way
            return remote(
                everything.at[slot],
                everything.at[slot],
                spread_send.at[a, way],
                spread_recv.at[a, way],
                distance,
                (lax.rem(row + sign + rows, rows), column),
            )

        def relay(distance):
            for way in range(2):
                sign = 1 - 2 * way
                source = row - sign * distance
                if distance > 0:

                    @pl.when(inside(source))
                    def _(way=way, source=source):
                        hop(way, distance - 1, source).wait_recv()

                if distance < rows - 1:

                    @pl.when(inside(source) & inside(row + sign))
                    def _(way=way, source=source):
                        hop(way, distance, source).start()

        relay(0)
        image[...] = 0.5 * own[...].astype(jnp.float32)
        extended[halo : halo + blocks] = own[...]
        for copy in halos:
            copy.wait()
        extended[0:halo] = left[...]
        extended[halo + blocks :] = right[...]

        @pl.loop(0, groups)
        def _(g):
            if a == 0:
                load(0, g).wait()
            near_group(sides, g, tables_ref, extended, near_ref, near_out, image)
            for distance in range(1, rows - 1):

                @pl.when(g == distance * groups // (rows - 1))
                def _(distance=distance):
                    relay(distance)

        relay(rows - 1)
        for way in range(2):
            sign = 1 - 2 * way
            for distance in range(rows - 1):
                source = row - sign * distance

                @pl.when(inside(source) & inside(row + sign))
                def _(way=way, source=source, distance=distance):
                    hop(way, distance, source).wait_send()

        between()
        if a == 0:
            for kind in (1, 2):

                @pl.loop(0, groups)
                def _(g, kind=kind):
                    load(kind, g).wait()

        far = functools.partial(
            far_group,
            sides,
            tables_ref=tables_ref,
            everything=everything,
            far_left=far_left,
            far_right=far_right,
            far_out=far_out,
        )

        def pair_copy(k, q):
            return remote(
                to_partner.at[q],
                from_partner.at[q],
                pair_send.at[a],
                pair_recv.at[a],
                k,
                (row, partner),
            )

        def chip_copy(k, q):
            return remote(
                to_chips.at[q],
                from_chips.at[chip],
                chip_send.at[a],
                chip_recv.at[a],
                k,
                (row, 2 * q + core),
            )

        @pl.loop(1, pairs + 1)
        def _(i):
            q = lax.rem(chip + i, pairs)
            k = i - 1
            to_partner[q] = far(2 * q + 1 - core)
            pair_copy(k, q).start()
            to_chips[q] = far(2 * q + core)
            pair_copy(k, q).wait_recv()
            to_chips[q] = to_chips[q] + from_partner[q]

            @pl.when(i < pairs)
            def _():
                chip_copy(k, q).start()

        image[...] += to_chips[chip]
        for i in range(1, pairs):
            source = lax.rem(chip + pairs - i, pairs)
            remote(
                to_chips.at[source],
                from_chips.at[source],
                chip_send.at[a],
                chip_recv.at[a],
                i - 1,
                (row, 2 * source + core),
            ).wait_recv()
            image[...] += from_chips[source]
        for i in range(1, pairs + 1):
            q = lax.rem(chip + i, pairs)
            pair_copy(i - 1, q).wait_send()
            if i < pairs:
                chip_copy(i - 1, q).wait_send()

    def all_sum(n, pairings):
        place = 0
        mine[n] = jnp.zeros(mine.shape[1:], jnp.float32)
        for one, two in pairings:
            for here in lanes:
                mine[n, place : place + 1] = jnp.sum(
                    one[:, here] * two[:, here], axis=0, keepdims=True
                )
                place += 1

        def copy(k, slot, peer):
            return remote(
                mine.at[n],
                parts.at[n, slot],
                sum_send.at[n],
                sum_recv.at[n],
                k,
                coordinates(peer, columns),
            )

        @pl.loop(1, count)
        def _(k):
            copy(k, me, lax.rem(me + k, count)).start()

        parts[n, me] = mine[n]

        @pl.loop(1, count)
        def _(k):
            source = lax.rem(me + count - k, count)
            copy(k, source, source).wait_recv()

        @pl.loop(1, count)
        def _(k):
            copy(k, me, lax.rem(me + k, count)).wait_send()

        return jnp.sum(jnp.sum(parts[n], axis=0), axis=1, keepdims=True) / panels

    def back(n, sent, landed):
        def copy(k, peer, slot):
            return remote(
                sent.at[peer],
                landed.at[slot],
                back_send.at[n],
                back_recv.at[n],
                k,
                coordinates(peer, columns),
            )

        def start(value):
            picked = split_dot(to_mesh_ref[...], value[...])
            for d in range(count):
                sent[d] = picked[d * capacity : (d + 1) * capacity]

            @pl.loop(1, count)
            def _(k):
                copy(k, lax.rem(me + k, count), me).start()

            landed[me] = sent[me]

        def wait():
            @pl.loop(1, count)
            def _(k):
                source = lax.rem(me + count - k, count)
                copy(k, source, source).wait_recv()

            @pl.loop(1, count)
            def _(k):
                copy(k, lax.rem(me + k, count), me).wait_send()

        return start, wait

    basis_start, basis_wait = back(0, outgoing, basis_back_ref)
    image_start, image_wait = back(1, outgoing_two, image_back_ref)

    own[...] = first_ref[...].astype(jnp.bfloat16)
    operate(0, lambda: None)
    project = all_sum(0, [(first_ref, image)])
    for s in range(sides):
        image[:, lanes[s]] = image[:, lanes[s]] - project[s : s + 1] * first_ref[:, lanes[s]]
    norm = jnp.sqrt(all_sum(1, [(image, image)]) + epsilon)
    for s in range(sides):
        value = image[:, lanes[s]] / norm[s : s + 1]
        basis[:, lanes[s]] = value
        own[:, lanes[s]] = value.astype(jnp.bfloat16)
    operate(1, lambda: basis_start(basis))
    image_start(image)
    projects = all_sum(2, [(first_ref, image), (basis, image)])

    def by_lane(column):
        shape = (column.shape[0], LANES)
        diagonal = lax.broadcasted_iota(jnp.int32, shape, 0) == lax.broadcasted_iota(
            jnp.int32, shape, 1
        )
        return jnp.sum(jnp.where(diagonal, column, 0.0), axis=0, keepdims=True)

    entries_ref[...] = jnp.zeros(entries_ref.shape, jnp.float32)
    found = (
        project[:sides],
        norm[:sides],
        projects[:sides],
        projects[sides : 2 * sides],
    )
    for place, value in enumerate(found):
        entries_ref[place : place + 1] = by_lane(value)

    def home(landed):
        for d in range(count):
            flat[d * capacity : (d + 1) * capacity] = landed[d]
        return split_dot(to_own_ref[...], flat[...])

    basis_wait()
    basis_ref[...] = home(basis_back_ref)
    image_wait()
    returned = home(image_back_ref)
    for s in range(sides):
        here = lanes[s]
        next_ref[:, here] = (
            returned[:, here]
            - projects[s : s + 1] * mesh_first_ref[:, here]
            - projects[sides + s : sides + s + 1] * basis_ref[:, here]
        )


def arnoldi(
    first, tables, to_mesh, to_own, mesh_first, near_blocks, far_left, far_right, rows, columns
):
    blocks, width = first.shape
    count = rows * columns
    groups = columns
    near_blocks = near_blocks.reshape(groups, -1, *near_blocks.shape[1:])
    far_left = far_left.reshape(groups, -1, *far_left.shape[1:])
    far_right = far_right.reshape(groups, -1, *far_right.shape[1:])
    halo = blocks // 4
    pairs = columns // 2
    dma = pltpu.SemaphoreType.DMA
    real, half = jnp.float32, jnp.bfloat16
    slots = (count, to_mesh.shape[0] // count, width)
    hbm = pl.BlockSpec(memory_space=pl.ANY)
    return pl.pallas_call(
        functools.partial(arnoldi_kernel, rows, columns),
        out_shape=[
            jax.ShapeDtypeStruct((blocks, width), real),
            jax.ShapeDtypeStruct((blocks, width), real),
            jax.ShapeDtypeStruct((8, LANES), real),
        ],
        in_specs=[VMEM] * 9 + [hbm] * 3,
        out_specs=[VMEM] * 3,
        scratch_shapes=[
            pltpu.VMEM((groups, 8, LANES), real),
            pltpu.VMEM(slots, real),
            pltpu.VMEM(slots, real),
            pltpu.VMEM((to_mesh.shape[0], width), real),
            pltpu.VMEM(near_blocks.shape, half),
            pltpu.VMEM(far_left.shape, half),
            pltpu.VMEM(far_right.shape, half),
            pltpu.VMEM((blocks, width), half),
            pltpu.VMEM((blocks, width), real),
            pltpu.VMEM((blocks, width), real),
            pltpu.VMEM((rows, blocks, width), half),
            pltpu.VMEM((blocks + 2 * halo, width), half),
            pltpu.VMEM((halo, width), half),
            pltpu.VMEM((halo, width), half),
            pltpu.VMEM((near_blocks.shape[1], width), real),
            pltpu.VMEM((far_left.shape[1], width), real),
            pltpu.VMEM((pairs, blocks, width), real),
            pltpu.VMEM((pairs, blocks, width), real),
            pltpu.VMEM((pairs, blocks, width), real),
            pltpu.VMEM((pairs, blocks, width), real),
            pltpu.VMEM(slots, real),
            pltpu.VMEM(slots, real),
            pltpu.VMEM((3, 8, LANES), real),
            pltpu.VMEM((3, count, 8, LANES), real),
            dma((3, groups)),
            dma((2, 2)),
            dma((2, 2)),
            dma((2, 2, rows - 1)),
            dma((2, 2, rows - 1)),
            dma((2, pairs)),
            dma((2, pairs)),
            dma((2, pairs)),
            dma((2, pairs)),
            dma((3, count)),
            dma((3, count)),
            dma((2, count)),
            dma((2, count)),
        ],
        compiler_params=pltpu.CompilerParams(
            collective_id=1, has_side_effects=True, vmem_limit_bytes=LIMIT
        ),
    )(first, *tables, to_mesh, to_own, mesh_first, near_blocks, far_left, far_right)


def body(
    right_side,
    cluster_of,
    near_rows,
    near_columns,
    near_blocks,
    far_rows,
    far_columns,
    far_rank,
    far_left,
    far_right,
):
    rows = lax.axis_size("row")
    columns = lax.axis_size("col")
    count = rows * columns
    blocks, sides, lanes = right_side.shape
    width = sides * lanes
    capacity = 2 * blocks // count
    panels = blocks * count * lanes
    far_count = far_rows.shape[0] // columns

    target = cluster_of // blocks
    place = cluster_of % blocks
    order = jnp.arange(blocks, dtype=jnp.int32)
    earlier = (target[None, :] == target[:, None]) & (order[None, :] < order[:, None])
    slot = target * capacity + jnp.sum(earlier.astype(jnp.int32), axis=1)
    slots = count * capacity
    to_slot = slot[None, :] == jnp.arange(slots, dtype=jnp.int32)[:, None]
    to_slot_f = to_slot.astype(jnp.float32)
    marks = jnp.sum(jnp.where(to_slot, place[None, :] + 1, 0), axis=1).astype(jnp.float32)

    lane = jnp.arange(lanes, dtype=jnp.int32)
    squares = jnp.sum(right_side * right_side, axis=(0, 2))
    half = lanes // 2
    step = half // sides
    square_lanes = jnp.repeat(squares, step)
    extra = jnp.concatenate(
        [
            jnp.broadcast_to(marks[:, None], (slots, half)),
            jnp.broadcast_to(square_lanes[None, :], (slots, half)),
        ],
        axis=1,
    )
    outgoing = jnp.dot(to_slot_f, right_side.reshape(blocks, width), precision=HIGH)
    arrived = exchange(
        jnp.concatenate([outgoing, extra], axis=1).reshape(count, capacity, width + lanes),
        rows,
        columns,
        0,
    )
    total = jnp.sum(arrived[:, 0, width + half :], axis=0).reshape(sides, step)[:, 0]
    side_norm = jnp.sqrt(total / panels + epsilon)
    arrived = arrived.reshape(slots, width + lanes)
    held = arrived[:, width].astype(jnp.int32) - 1
    from_slot = held[None, :] == order[:, None]
    to_cluster = from_slot.astype(jnp.float32)
    norm_lanes = jnp.repeat(side_norm, lanes)
    first = jnp.dot(to_cluster, arrived[:, :width], precision=HIGH) / norm_lanes[None, :]


    tables = [
        values.reshape(columns, -1)
        for values in (near_columns, near_rows, far_columns, far_rows, far_rank)
    ]
    to_mesh = (held[:, None] == order[None, :]).astype(jnp.bfloat16)
    to_own = (slot[:, None] == jnp.arange(slots, dtype=jnp.int32)[None, :]).astype(jnp.bfloat16)
    mesh_first = right_side.reshape(blocks, width) / norm_lanes[None, :]
    basis, following, entries = arnoldi(
        first,
        tables,
        to_mesh,
        to_own,
        mesh_first,
        near_blocks,
        far_left,
        far_right,
        rows,
        columns,
    )
    second_basis = basis.reshape(blocks, sides, lanes)
    next_vector = following.reshape(blocks, sides, lanes)
    hessenberg = jnp.concatenate([side_norm[None, :], entries[:4, :sides]], axis=0)
    return (second_basis, next_vector, hessenberg)


def solution(mesh):
    vector = P(("row", "col"), None, None)
    table = P(("row", "col"))
    placed = (vector, table, table, table, vector, table, table, table, vector, vector)
    return jax.shard_map(
        body,
        mesh=mesh,
        in_specs=placed,
        out_specs=(vector, vector, P()),
        check_vma=False,
    )
```
